512 devices in a mesh: ctx: 64 (over x, z), head: 8 (over y, core).
Axes of the slice: x: 4, y: 4, z: 16, core: 2. Of those that a mesh axis runs over, the one named last changes fastest.
Arguments:
- queries: bfloat16 [65536, 4096], P('ctx', 'head'), may hold values from -8 to 8
- span_key_array: bfloat16 [65536, 1024], P('ctx', 'head'), may hold values from -8 to 8
- span_value_array: bfloat16 [65536, 1024], P('ctx', 'head'), may hold values from -6 to 6
- cached_key_array: bfloat16 [262144, 1024], P('ctx', 'head'), may hold values from -8 to 8
- cached_value_array: bfloat16 [262144, 1024], P('ctx', 'head'), may hold values from -6 to 6
- chosen: int32 [128, 8, 3], P('ctx', 'head'), may hold values from 0 to 511, as said below
Outputs:
- attended: bfloat16 [65536, 4096], P(('ctx', 'head'))
The draws below stay inside these ranges and needn't reach their ends.
Inputs may be any that keep to these rules, and one draw needn't show every extreme that they name: For each query block and KV head the 3 numbers are cache blocks on 3 different devices (block b lies on index b // 8 of ctx). For one KV head, over all query blocks, at most 2 of the 8 blocks of one device are ever chosen, and exactly 2 on some device.
All inputs are finite; a program needn't handle non-finite values.
Results may differ from the reference program's by a relative error of at most 0.0049.
Values may be sent and summed in bfloat16 or wider, within the bound.
A program may use at most 64 MiB of HBM per device.

```python
import math
import jax
import jax.numpy as jnp
from jax import lax

HEAD_SIZE = 128
QUERY_HEADS = 32
KEY_VALUE_HEADS = 8
BLOCK_TOKENS = 512
CHOSEN_COUNT = 3
HOT_BLOCK_LIMIT = 2
DEVICE_BLOCKS = 8
SPAN_ROWS = 65536
CACHE_TOKENS = 262144
QUERY_BLOCKS = 128
CACHE_BLOCKS = 512
N_CTX = 64


def drawn_rows(key, row_total, col_total):
    return jnp.clip(jax.random.normal(key, (row_total, col_total), jnp.float32), -6.0, 6.0)


def draw_queries(key, part):
    key = jax.random.fold_in(key, 11)
    return drawn_rows(key, SPAN_ROWS, QUERY_HEADS * HEAD_SIZE).astype(jnp.bfloat16)


def draw_span_key_array(key, part):
    key = jax.random.fold_in(key, 13)
    return drawn_rows(key, SPAN_ROWS, KEY_VALUE_HEADS * HEAD_SIZE).astype(jnp.bfloat16)


def draw_cached_key_array(key, part):
    key = jax.random.fold_in(key, 12)
    return drawn_rows(key, CACHE_TOKENS, KEY_VALUE_HEADS * HEAD_SIZE).astype(jnp.bfloat16)


def draw_chosen(key, part):
    key = jax.random.fold_in(key, 14)
    random_subkeys = jax.random.split(key, 6)
    popular_owner = jax.random.randint(random_subkeys[0], (KEY_VALUE_HEADS,), 0, N_CTX)
    shuffled_blocks = jax.vmap(lambda single_key: jax.random.permutation(single_key, QUERY_BLOCKS))(jax.random.split(random_subkeys[1], KEY_VALUE_HEADS))
    shuffled_blocks = jnp.transpose(shuffled_blocks).astype(jnp.int32)
    first_owner = shuffled_blocks % N_CTX
    first_slot = shuffled_blocks // N_CTX % HOT_BLOCK_LIMIT

    def skewed(single_key):
        candidate_blocks = jax.random.randint(single_key, (3, QUERY_BLOCKS, KEY_VALUE_HEADS), 0, N_CTX)
        return (jnp.min(candidate_blocks, axis=0) + popular_owner[None, :]) % N_CTX
    owner_two = skewed(random_subkeys[2])
    owner_two = jnp.where(owner_two == first_owner, (owner_two + 1) % N_CTX, owner_two)
    owner_three = skewed(random_subkeys[3])
    collides = (owner_three == first_owner) | (owner_three == owner_two)
    owner_three = jnp.where(collides, (owner_three + 1) % N_CTX, owner_three)
    collides = (owner_three == first_owner) | (owner_three == owner_two)
    owner_three = jnp.where(collides, (owner_three + 1) % N_CTX, owner_three)
    slot_sample = jax.random.randint(random_subkeys[4], (2, QUERY_BLOCKS, KEY_VALUE_HEADS), 0, HOT_BLOCK_LIMIT)
    eligible_mask = jax.vmap(lambda single_key: jax.random.permutation(single_key, DEVICE_BLOCKS))(jax.random.split(random_subkeys[5], N_CTX * KEY_VALUE_HEADS))
    eligible_mask = eligible_mask.reshape(N_CTX, KEY_VALUE_HEADS, DEVICE_BLOCKS)[:, :, :HOT_BLOCK_LIMIT].astype(jnp.int32)
    head_index_list = jnp.arange(KEY_VALUE_HEADS)[None, :]
    block_one = first_owner * DEVICE_BLOCKS + eligible_mask[first_owner, head_index_list, first_slot]
    block_two = owner_two * DEVICE_BLOCKS + eligible_mask[owner_two, head_index_list, slot_sample[0]]
    block_three = owner_three * DEVICE_BLOCKS + eligible_mask[owner_three, head_index_list, slot_sample[1]]
    return jnp.stack([block_one, block_two, block_three], axis=2).astype(jnp.int32)


def block_levels(stream_key, extent, pieces, smallest, top_value):
    loudness = 1.0
    for axis_at, shards_of in pieces:
        draws = jax.random.uniform(jax.random.fold_in(jax.random.fold_in(stream_key, 6), axis_at), (shards_of,), jnp.float32, smallest / len(pieces), top_value / len(pieces))
        loudness = loudness * jnp.repeat(jnp.exp(draws), extent[axis_at] // shards_of).reshape((-1,) + (1,) * (len(extent) - 1 - axis_at))
    return loudness


def centred(key, dims, deviation, reach, cuts=(), held_as=jnp.bfloat16):
    values = jax.random.normal(key, dims, jnp.float32) * deviation
    if len(cuts) > 0:
        values = block_levels(key, dims, cuts, -0.22, 0.18) * values
    return jnp.clip(values, min=-reach, max=reach).astype(held_as)


def setup_inputs(seed: int = 0) -> dict:
    seeds = jax.random.split(jax.random.key(seed), 7)
    return {
        "queries": draw_queries(jax.random.fold_in(seeds[6], 71), 0),
        "span_key_array": draw_span_key_array(jax.random.fold_in(seeds[6], 71), 0),
        "span_value_array": centred(seeds[2], (SPAN_ROWS, KEY_VALUE_HEADS * HEAD_SIZE), 1.0, 6.0, ((0, 64), (1, 8))),
        "cached_key_array": draw_cached_key_array(jax.random.fold_in(seeds[6], 71), 0),
        "cached_value_array": centred(seeds[4], (CACHE_TOKENS, KEY_VALUE_HEADS * HEAD_SIZE), 1.0, 6.0, ((0, 64), (1, 8))),
        "chosen": draw_chosen(jax.random.fold_in(seeds[6], 71), 0),
    }


def reference(queries, span_key_array, span_value_array, cached_key_array, cached_value_array, chosen):
    group_share = QUERY_HEADS // KEY_VALUE_HEADS
    inv_root = 1.0 / math.sqrt(HEAD_SIZE)
    query_block_rows = queries.reshape(QUERY_BLOCKS, BLOCK_TOKENS, KEY_VALUE_HEADS, group_share, HEAD_SIZE)
    nearby_keys = span_key_array.reshape(QUERY_BLOCKS, BLOCK_TOKENS, KEY_VALUE_HEADS, HEAD_SIZE)
    nearby_values = span_value_array.reshape(QUERY_BLOCKS, BLOCK_TOKENS, KEY_VALUE_HEADS, HEAD_SIZE)
    kept_keys = cached_key_array.reshape(CACHE_BLOCKS, BLOCK_TOKENS, KEY_VALUE_HEADS, HEAD_SIZE)
    kept_values = cached_value_array.reshape(CACHE_BLOCKS, BLOCK_TOKENS, KEY_VALUE_HEADS, HEAD_SIZE)
    causal = jnp.arange(BLOCK_TOKENS)[:, None] >= jnp.arange(BLOCK_TOKENS)[None, :]
    visible = jnp.concatenate([causal, jnp.ones((BLOCK_TOKENS, CHOSEN_COUNT * BLOCK_TOKENS), dtype=bool)], axis=1)
    head_index_list = jnp.arange(KEY_VALUE_HEADS, dtype=jnp.int32)[:, None]

    def one_block(inputs):
        block_queries, block_keys, block_values, picked_blocks = inputs
        picked_blocks = picked_blocks.astype(jnp.int32)
        distant_keys = kept_keys[picked_blocks, :, head_index_list, :].reshape(KEY_VALUE_HEADS, CHOSEN_COUNT * BLOCK_TOKENS, HEAD_SIZE)
        distant_values = kept_values[picked_blocks, :, head_index_list, :].reshape(KEY_VALUE_HEADS, CHOSEN_COUNT * BLOCK_TOKENS, HEAD_SIZE)
        all_keys = jnp.concatenate([jnp.transpose(block_keys, (1, 0, 2)), distant_keys], axis=1).astype(jnp.float32)
        all_values = jnp.concatenate([jnp.transpose(block_values, (1, 0, 2)), distant_values], axis=1).astype(jnp.float32)
        scores = jnp.einsum('igrh,gjh->grij', block_queries.astype(jnp.float32), all_keys) * inv_root
        scores = jnp.where(visible, scores, -jnp.inf)
        scores = scores - lax.optimization_barrier(jnp.max(scores, axis=-1, keepdims=True))
        exponent = jnp.exp(scores)
        weights = (exponent / lax.optimization_barrier(jnp.sum(exponent, axis=-1, keepdims=True))).astype(jnp.bfloat16)
        result = jnp.einsum('grij,gjh->igrh', weights.astype(jnp.float32), all_values)
        return result.astype(jnp.bfloat16).reshape(BLOCK_TOKENS, QUERY_HEADS * HEAD_SIZE)
    attended = lax.map(one_block, (query_block_rows, nearby_keys, nearby_values, chosen))
    return attended.reshape(QUERY_BLOCKS * BLOCK_TOKENS, QUERY_HEADS * HEAD_SIZE)
```

```python
import functools
import math

import jax
import jax.numpy as jnp
from jax import lax
from jax.experimental import pallas as pl
from jax.experimental.pallas import tpu as pltpu
from jax.sharding import PartitionSpec as P

HEAD_SIZE = 128
BLOCK = 512
PICKS = 3
HOT = 2
NX, NZ = 4, 16
HALF = NZ // 2
REACH = HALF // 2
N_CTX = NX * NZ
N_HEAD = 8
SLICES = NX * HALF
ROWS = BLOCK // SLICES
GROUP = 4
Q_BLOCKS = 2
DEV_BLOCKS = 8
LIST = BLOCK * (PICKS + 1)
CHUNK = 256
LOG2_SCALE = math.log2(math.e) / math.sqrt(HEAD_SIZE)
BIG = 1 << 20
MESH = pl.DeviceIdType.MESH


def dot_rows(left, right):
    return lax.dot_general(
        left, right, (((1,), (1,)), ((), ())), preferred_element_type=jnp.float32
    )


def remote(src, dst, send_sem, recv_sem, axis, peer):
    return pltpu.make_async_remote_copy(
        src_ref=src,
        dst_ref=dst,
        send_sem=send_sem,
        recv_sem=recv_sem,
        device_id={axis: peer},
        device_id_type=MESH,
    )


def drain(ref, sem):
    pltpu.make_async_copy(ref, ref, sem).wait()


def kernel(
    q_hbm, ks_hbm, vs_hbm, kc_hbm, vc_hbm, chosen_ref, out_hbm,
    q_v, ks_v, vs_v, cache_k, cache_w, hot_v, table_k, table_w, send_v, far_v,
    row_v, all_v, index_v, index_s, weights_v, out_v,
    load_sem, index_sem, ch_send, ch_recv, p1_send, p1_recv, p2_send, p2_recv,
    out_send, out_recv, out_local,
):
    me = lax.axis_index("ctx")
    head = lax.axis_index("head")
    mx, mz = me // NZ, me % NZ
    place = mx * HALF + mz % HALF
    caches, tables = (cache_k, cache_w), (table_k, table_w)

    loads = [
        pltpu.make_async_copy(kc_hbm, cache_k, load_sem.at[0]),
        pltpu.make_async_copy(vc_hbm, cache_w, load_sem.at[1]),
        pltpu.make_async_copy(q_hbm, q_v, load_sem.at[2]),
        pltpu.make_async_copy(ks_hbm, ks_v, load_sem.at[3]),
        pltpu.make_async_copy(vs_hbm, vs_v, load_sem.at[4]),
    ]
    for load in loads:
        load.start()

    barrier = pltpu.get_barrier_semaphore()

    @pl.loop(1, N_CTX)
    def _(i):
        pl.semaphore_signal(
            barrier, inc=1, device_id={"ctx": (me + i) % N_CTX}, device_id_type=MESH
        )

    @pl.loop(1, N_HEAD)
    def _(i):
        pl.semaphore_signal(
            barrier, inc=1, device_id={"head": (head + i) % N_HEAD}, device_id_type=MESH
        )

    lane = lax.broadcasted_iota(jnp.int32, (1, 128), 1)
    mine = jnp.full((1, 128), -1, jnp.int32)
    for b in range(Q_BLOCKS):
        for j in range(PICKS):
            mine = jnp.where(lane == b * PICKS + j, chosen_ref[b, 0, j], mine)
    row_v[0] = mine
    pl.semaphore_wait(barrier, N_CTX - 1 + N_HEAD - 1)

    @pl.loop(1, N_CTX)
    def _(i):
        remote(row_v.at[0], all_v.at[me], ch_send, ch_recv, "ctx", (me + i) % N_CTX).start()

    all_v[me] = mine
    drain(all_v.at[pl.ds(0, N_CTX - 1)], ch_recv)
    picked = all_v[...].reshape(N_CTX, 128)
    owner = jnp.where(picked < 0, -1, picked // DEV_BLOCKS)
    here = owner == me
    low = jnp.min(jnp.where(here, picked, BIG))
    high = jnp.max(jnp.where(here, picked, -1))
    first = me * DEV_BLOCKS
    low = jnp.clip(low - first, 0, DEV_BLOCKS - 1)
    high = jnp.clip(high - first, 0, DEV_BLOCKS - 1)

    def spread(t):
        loads[t].wait()
        hot_v[t, 0] = caches[t][low]
        hot_v[t, 1] = caches[t][high]

        @pl.loop(1, N_CTX)
        def _(i):
            x = (mx + i // NZ) % NX
            z = (mz + i * 5) % NZ
            at = pl.multiple_of((x * HALF + z % HALF) * ROWS, ROWS)
            remote(
                hot_v.at[t, :, pl.ds(at, ROWS)],
                tables[t].at[pl.ds(me * HOT, HOT)],
                p1_send.at[t], p1_recv.at[t], "ctx", x * NZ + z,
            ).start()

        at = pl.multiple_of(place * ROWS, ROWS)
        tables[t][pl.ds(me * HOT, HOT)] = hot_v[t, :, pl.ds(at, ROWS)]

    spread(0)
    spread(1)

    lane_c = lax.broadcasted_iota(jnp.int32, (N_CTX, 128), 1)
    lows = jnp.full((1, 128), BIG, jnp.int32)
    for e in range(Q_BLOCKS * PICKS):
        hit = owner[:, e : e + 1] == lane_c
        lows = jnp.minimum(
            lows, jnp.min(jnp.where(hit, picked[:, e : e + 1], BIG), axis=0, keepdims=True)
        )
    index = jnp.zeros((N_CTX, 128), jnp.int32)
    for e in range(Q_BLOCKS * PICKS):
        hit = owner[:, e : e + 1] == lane_c
        least = jnp.min(jnp.where(hit, lows, BIG), axis=1, keepdims=True)
        spot = owner[:, e : e + 1] * HOT + (picked[:, e : e + 1] != least).astype(jnp.int32)
        index = jnp.where(lane_c == e, spot, index)
    index_v[...] = index
    to_scalar = pltpu.make_async_copy(index_v, index_s, index_sem)
    to_scalar.start()
    to_scalar.wait()

    def fill(t, b, peer, ref):
        for j in range(PICKS):
            ref[pl.ds(j * ROWS, ROWS)] = tables[t][index_s[peer, b * PICKS + j]]

    def deliver(t, b):
        fill(t, b, me, far_v.at[t, b, place])
        stay = REACH - 1 + b

        @pl.loop(0, SLICES - 1)
        def _(i):
            i = i + jnp.where(i >= stay, 1, 0)
            x = (mx + i // HALF) % NX
            z = (mz + i % HALF - stay + NZ) % NZ
            peer = x * NZ + z
            fill(t, b, peer, send_v.at[t, b, i])
            remote(
                send_v.at[t, b, i], far_v.at[t, b, place],
                p2_send.at[t], p2_recv.at[t, b], "ctx", peer,
            ).start()

    def hold(t):
        drain(tables[t].at[pl.ds(0, HOT * (N_CTX - 1))], p1_recv.at[t])
        for b in range(Q_BLOCKS):
            deliver(t, b)

    hold(0)
    hold(1)
    for load in loads[2:]:
        load.wait()

    def softmax(b):
        drain(far_v.at[0, b, pl.ds(0, SLICES - 1)], p2_recv.at[0, b])
        far_keys = far_v[0, b].reshape(PICKS * BLOCK, HEAD_SIZE)

        @pl.loop(0, GROUP)
        def _(h):
            for r in range(BLOCK // CHUNK):
                query = q_v[
                    b * BLOCK + r * CHUNK : b * BLOCK + (r + 1) * CHUNK,
                    pl.ds(pl.multiple_of(h * HEAD_SIZE, HEAD_SIZE), HEAD_SIZE),
                ]
                near = dot_rows(query, ks_v[b * BLOCK : (b + 1) * BLOCK])
                below = (
                    r * CHUNK + lax.broadcasted_iota(jnp.int32, (CHUNK, BLOCK), 0)
                    >= lax.broadcasted_iota(jnp.int32, (CHUNK, BLOCK), 1)
                )
                near = jnp.where(below, near, -jnp.inf)
                far = dot_rows(query, far_keys)
                top = jnp.maximum(
                    jnp.max(near, axis=1, keepdims=True), jnp.max(far, axis=1, keepdims=True)
                )
                near = jnp.exp2((near - top) * LOG2_SCALE)
                far = jnp.exp2((far - top) * LOG2_SCALE)
                share = 1.0 / (
                    jnp.sum(near, axis=1, keepdims=True) + jnp.sum(far, axis=1, keepdims=True)
                )
                rows = pl.ds(r * CHUNK, CHUNK)
                weights_v[b, h, rows, 0:BLOCK] = (near * share).astype(jnp.bfloat16)
                weights_v[b, h, rows, BLOCK:LIST] = (far * share).astype(jnp.bfloat16)

    def combine(b):
        drain(far_v.at[1, b, pl.ds(0, SLICES - 1)], p2_recv.at[1, b])
        far_values = far_v[1, b].reshape(PICKS * BLOCK, HEAD_SIZE)
        near_values = vs_v[b * BLOCK : (b + 1) * BLOCK]

        @pl.loop(0, GROUP)
        def _(h):
            total = jnp.dot(
                weights_v[b, h, :, 0:BLOCK], near_values, preferred_element_type=jnp.float32
            ) + jnp.dot(
                weights_v[b, h, :, BLOCK:LIST], far_values, preferred_element_type=jnp.float32
            )
            out_v[
                pl.ds(b * BLOCK, BLOCK), pl.ds(pl.multiple_of(h * HEAD_SIZE, HEAD_SIZE), HEAD_SIZE)
            ] = total.astype(jnp.bfloat16)

        for t in range(b * GROUP, (b + 1) * GROUP):
            give(t, True)

    def give(t, start):
        width = GROUP * HEAD_SIZE
        part = out_v.at[pl.ds(t * 128, 128)]
        spot = out_hbm.at[:, pl.ds(pl.multiple_of(head * width, width), width)]

        @pl.when(t != head)
        def _():
            copy = remote(part, spot, out_send.at[t], out_recv, "head", t)
            if start:
                copy.start()
            else:
                copy.wait_send()

        @pl.when(t == head)
        def _():
            copy = pltpu.make_async_copy(part, spot, out_local)
            if start:
                copy.start()
            else:
                copy.wait()

    for b in range(Q_BLOCKS):
        softmax(b)
    for b in range(Q_BLOCKS):
        combine(b)
    drain(out_hbm.at[:, pl.ds(0, (N_HEAD - 1) * GROUP * HEAD_SIZE)], out_recv)
    for t in range(N_HEAD):
        give(t, False)
    drain(all_v.at[pl.ds(0, N_CTX - 1)], ch_send)
    for t in range(2):
        drain(tables[t].at[pl.ds(0, HOT * (N_CTX - 1))], p1_send.at[t])
        drain(send_v.at[t, :, pl.ds(0, SLICES - 1)], p2_send.at[t])


def shards(queries, span_keys, span_values, cached_keys, cached_values, chosen):
    rows, width = queries.shape
    bf16 = jnp.bfloat16
    anywhere = pl.BlockSpec(memory_space=pl.ANY)
    dma = pltpu.SemaphoreType.DMA
    return pl.pallas_call(
        kernel,
        out_shape=jax.ShapeDtypeStruct((rows // N_HEAD, width * N_HEAD), bf16),
        in_specs=[anywhere] * 5 + [pl.BlockSpec(memory_space=pltpu.SMEM)],
        out_specs=anywhere,
        scratch_shapes=[
            pltpu.VMEM((rows, width), bf16),
            pltpu.VMEM((rows, HEAD_SIZE), bf16),
            pltpu.VMEM((rows, HEAD_SIZE), bf16),
            pltpu.VMEM((DEV_BLOCKS, BLOCK, HEAD_SIZE), bf16),
            pltpu.VMEM((DEV_BLOCKS, BLOCK, HEAD_SIZE), bf16),
            pltpu.VMEM((2, HOT, BLOCK, HEAD_SIZE), bf16),
            pltpu.VMEM((HOT * N_CTX, ROWS, HEAD_SIZE), bf16),
            pltpu.VMEM((HOT * N_CTX, ROWS, HEAD_SIZE), bf16),
            pltpu.VMEM((2, Q_BLOCKS, SLICES, PICKS * ROWS, HEAD_SIZE), bf16),
            pltpu.VMEM((2, Q_BLOCKS, SLICES, PICKS * ROWS, HEAD_SIZE), bf16),
            pltpu.VMEM((1, 1, 128), jnp.int32),
            pltpu.VMEM((N_CTX, 1, 128), jnp.int32),
            pltpu.VMEM((N_CTX, 128), jnp.int32),
            pltpu.SMEM((N_CTX, 128), jnp.int32),
            pltpu.VMEM((Q_BLOCKS, GROUP, BLOCK, LIST), bf16),
            pltpu.VMEM((rows, width), bf16),
            dma((5,)), dma, dma, dma, dma((2,)), dma((2,)), dma((2,)), dma((2, 2)),
            dma((N_HEAD,)), dma, dma,
        ],
        compiler_params=pltpu.CompilerParams(
            collective_id=0, has_side_effects=True, vmem_limit_bytes=56 << 20
        ),
        cost_estimate=pl.CostEstimate(
            flops=4 * rows * GROUP * LIST * HEAD_SIZE,
            bytes_accessed=8 << 20,
            transcendentals=rows * GROUP * LIST,
        ),
    )(
        queries, span_keys, span_values,
        cached_keys.reshape(DEV_BLOCKS, BLOCK, HEAD_SIZE),
        cached_values.reshape(DEV_BLOCKS, BLOCK, HEAD_SIZE),
        chosen,
    )


def solution(mesh):
    placed = (P("ctx", "head"),) * 5 + (P("ctx", "head", None),)
    return jax.shard_map(
        shards, mesh=mesh, in_specs=placed, out_specs=P(("ctx", "head"), None), check_vma=False
    )
```

```python
import functools
import math

import jax
import jax.numpy as jnp
from jax import lax
from jax.experimental import pallas as pl
from jax.experimental.pallas import tpu as pltpu
from jax.sharding import PartitionSpec as P

HEAD_SIZE = 128
BLOCK = 512
PICKS = 3
HOT = 2
NX, NZ = 4, 16
HALF = NZ // 2
FAR_X = (2, 1, 3)
REACH = HALF // 2
N_CTX = NX * NZ
N_HEAD = 8
SLICES = NX * HALF
ROWS = BLOCK // SLICES
COLUMN = BLOCK // NX
GROUP = 4
OWN_ROWS = 128
Q_BLOCKS = 2
DEV_BLOCKS = 8
LIST = BLOCK * (PICKS + 1)
CHUNK = 256
LOG2_SCALE = math.log2(math.e) / math.sqrt(HEAD_SIZE)
BIG = 1 << 20
MESH = pl.DeviceIdType.MESH


def dot_rows(left, right):
    return lax.dot_general(
        left, right, (((1,), (1,)), ((), ())), preferred_element_type=jnp.float32
    )


def remote(src, dst, send_sem, recv_sem, axis, peer):
    return pltpu.make_async_remote_copy(
        src_ref=src,
        dst_ref=dst,
        send_sem=send_sem,
        recv_sem=recv_sem,
        device_id={axis: peer},
        device_id_type=MESH,
    )


def drain(ref, sem):
    pltpu.make_async_copy(ref, ref, sem).wait()


def kernel(
    q_hbm, ks_hbm, vs_hbm, kc_hbm, vc_hbm, chosen_ref, out_ref,
    q_v, ks_v, vs_v, cache_k, cache_w, hot_v, column_v, table_k, table_w, send_v, relay_v, far_v,
    row_v, all_v, index_v, index_s, weights_v, out_v,
    load_sem, index_sem, ch_send, ch_recv, p1_send, p1_recv, p2_send, p2_recv,
    x1_recv, x2_recv, out_send, out_recv, out_local,
):
    me = lax.axis_index("ctx")
    head = lax.axis_index("head")
    mx, mz = me // NZ, me % NZ
    mine_at = mz % HALF
    caches, tables = (cache_k, cache_w), (table_k, table_w)

    def along_x(d):
        return (mx + d) % NX * NZ + mz

    def along_z(d):
        return mx * NZ + (mz + d) % NZ

    loads = [
        pltpu.make_async_copy(kc_hbm, cache_k, load_sem.at[0]),
        pltpu.make_async_copy(vc_hbm, cache_w, load_sem.at[1]),
        pltpu.make_async_copy(q_hbm, q_v, load_sem.at[2]),
        pltpu.make_async_copy(ks_hbm, ks_v, load_sem.at[3]),
        pltpu.make_async_copy(vs_hbm, vs_v, load_sem.at[4]),
    ]
    for load in loads[:2]:
        load.start()

    def far_first(i):
        return HALF + (i + 1) // 2 * (1 - i % 2 * 2)

    barrier = pltpu.get_barrier_semaphore()

    def greet(axis, peer):
        pl.semaphore_signal(barrier, inc=1, device_id={axis: peer}, device_id_type=MESH)

    @pl.loop(0, NZ - 1)
    def _(i):
        greet("ctx", along_z(far_first(i)))

    for d in FAR_X:
        greet("ctx", along_x(d))

    @pl.loop(1, N_HEAD)
    def _(i):
        greet("head", (head + i) % N_HEAD)

    lane = lax.broadcasted_iota(jnp.int32, (1, 128), 1)
    mine = jnp.full((1, 128), -1, jnp.int32)
    for b in range(Q_BLOCKS):
        for j in range(PICKS):
            mine = jnp.where(lane == b * PICKS + j, chosen_ref[b, 0, j], mine)
    row_v[0] = mine
    all_v[me] = mine
    pl.semaphore_wait(barrier, NZ - 1 + NX - 1 + N_HEAD - 1)

    @pl.loop(0, NZ - 1)
    def _(i):
        remote(
            row_v.at[0], all_v.at[me], ch_send.at[0], ch_recv.at[0], "ctx",
            along_z(far_first(i)),
        ).start()

    drain(all_v.at[pl.ds(0, NZ - 1)], ch_recv.at[0])
    column = all_v.at[pl.ds(mx * NZ, NZ)]

    for d in FAR_X:
        remote(column, column, ch_send.at[1], ch_recv.at[1], "ctx", along_x(d)).start()

    drain(all_v.at[pl.ds(0, (NX - 1) * NZ)], ch_recv.at[1])
    picked = all_v[...].reshape(N_CTX, 128)
    owner = jnp.where(picked < 0, -1, picked // DEV_BLOCKS)
    here = owner == me
    low = jnp.min(jnp.where(here, picked, BIG))
    high = jnp.max(jnp.where(here, picked, -1))
    first = me * DEV_BLOCKS
    low = jnp.clip(low - first, 0, DEV_BLOCKS - 1)
    high = jnp.clip(high - first, 0, DEV_BLOCKS - 1)

    def spread_x(t):
        loads[t].wait()
        hot_v[t, 0] = caches[t][low]
        hot_v[t, 1] = caches[t][high]
        for d in range(1, NX):
            at = pl.multiple_of((mx + d) % NX * COLUMN, COLUMN)
            remote(
                hot_v.at[t, :, pl.ds(at, COLUMN)],
                column_v.at[t, pl.ds((NX - d) * HOT, HOT)],
                p1_send.at[t], x1_recv.at[t], "ctx", along_x(d),
            ).start()
        at = pl.multiple_of(mx * COLUMN, COLUMN)
        column_v[t, 0:HOT] = hot_v[t, :, pl.ds(at, COLUMN)]

    def spread_z(t, start, count):
        @pl.loop(1, NZ)
        def _(i):
            at = pl.multiple_of((mz + i * 5) % HALF * ROWS, ROWS)
            remote(
                column_v.at[t, pl.ds(start, count), pl.ds(at, ROWS)],
                tables[t].at[pl.ds(mz * HOT * NX + start, count)],
                p1_send.at[t], p1_recv.at[t], "ctx", along_z(i * 5),
            ).start()

        at = pl.multiple_of(mine_at * ROWS, ROWS)
        tables[t][pl.ds(mz * HOT * NX + start, count)] = column_v[
            t, pl.ds(start, count), pl.ds(at, ROWS)
        ]

    spread_x(0)
    spread_z(0, 0, HOT)
    spread_x(1)
    drain(column_v.at[0, pl.ds(HOT, HOT * (NX - 1))], x1_recv.at[0])
    spread_z(0, HOT, HOT * (NX - 1))
    drain(column_v.at[1, pl.ds(HOT, HOT * (NX - 1))], x1_recv.at[1])
    spread_z(1, 0, HOT * NX)

    for load in loads[2:]:
        load.start()

    lane_c = lax.broadcasted_iota(jnp.int32, (N_CTX, 128), 1)
    lows = jnp.full((1, 128), BIG, jnp.int32)
    for e in range(Q_BLOCKS * PICKS):
        hit = owner[:, e : e + 1] == lane_c
        lows = jnp.minimum(
            lows, jnp.min(jnp.where(hit, picked[:, e : e + 1], BIG), axis=0, keepdims=True)
        )
    index = jnp.zeros((N_CTX, 128), jnp.int32)
    for e in range(Q_BLOCKS * PICKS):
        at = owner[:, e : e + 1]
        hit = at == lane_c
        least = jnp.min(jnp.where(hit, lows, BIG), axis=1, keepdims=True)
        later = (picked[:, e : e + 1] != least).astype(jnp.int32)
        spot = (at % NZ * NX + (at // NZ + NX - mx) % NX) * HOT + later
        index = jnp.where(lane_c == e, spot, index)
    index_v[...] = index
    to_scalar = pltpu.make_async_copy(index_v, index_s, index_sem)
    to_scalar.start()
    to_scalar.wait()

    def fill(t, b, peer, ref):
        for j in range(PICKS):
            ref[pl.ds(j * ROWS, ROWS)] = tables[t][index_s[peer, b * PICKS + j]]

    def z_shift(b, k):
        return k + NZ - (REACH - 1 + b)

    def deliver_x(t, b):
        @pl.loop(0, HALF)
        def _(k):
            fill(t, b, along_z(z_shift(b, k)), relay_v.at[t, b, 0, k])

        for d in range(1, NX):
            @pl.loop(0, HALF)
            def _(k):
                peer = (mx + d) % NX * NZ + (mz + z_shift(b, k)) % NZ
                fill(t, b, peer, send_v.at[t, b, d - 1, k])

            remote(
                send_v.at[t, b, d - 1], relay_v.at[t, b, NX - d],
                p2_send.at[t], x2_recv.at[t, b], "ctx", along_x(d),
            ).start()

    def deliver_z(t, b):
        drain(relay_v.at[t, b, pl.ds(1, NX - 1)], x2_recv.at[t, b])
        stay = REACH - 1 + b

        @pl.loop(0, HALF - 1)
        def _(i):
            k = (stay + 3 + i * 3) % HALF
            remote(
                relay_v.at[t, b, :, k], far_v.at[t, b, mine_at],
                p2_send.at[t], p2_recv.at[t, b], "ctx", along_z(z_shift(b, k)),
            ).start()

        far_v[t, b, mine_at] = relay_v[t, b, :, stay]

    lead = 1 - head // (N_HEAD // 2)
    order = (lead, 1 - lead)
    for t in range(2):
        drain(tables[t].at[pl.ds(0, HOT * NX * (NZ - 1))], p1_recv.at[t])
        for b in order:
            deliver_x(t, b)
        for b in order:
            deliver_z(t, b)
    for load in loads[2:]:
        load.wait()

    def softmax(b):
        drain(far_v.at[0, b, pl.ds(0, HALF - 1)], p2_recv.at[0, b])
        far_keys = far_v[0, b].reshape(PICKS * BLOCK, HEAD_SIZE)
        near_keys = ks_v[pl.ds(pl.multiple_of(b * BLOCK, BLOCK), BLOCK)]

        @pl.loop(0, GROUP)
        def _(h):
            for r in range(BLOCK // CHUNK):
                query = q_v[
                    pl.ds(pl.multiple_of(b * BLOCK + r * CHUNK, CHUNK), CHUNK),
                    pl.ds(pl.multiple_of(h * HEAD_SIZE, HEAD_SIZE), HEAD_SIZE),
                ]
                near = dot_rows(query, near_keys)
                below = (
                    r * CHUNK + lax.broadcasted_iota(jnp.int32, (CHUNK, BLOCK), 0)
                    >= lax.broadcasted_iota(jnp.int32, (CHUNK, BLOCK), 1)
                )
                near = jnp.where(below, near, -jnp.inf)
                far = dot_rows(query, far_keys)
                top = jnp.maximum(
                    jnp.max(near, axis=1, keepdims=True), jnp.max(far, axis=1, keepdims=True)
                )
                near = jnp.exp2((near - top) * LOG2_SCALE)
                far = jnp.exp2((far - top) * LOG2_SCALE)
                share = 1.0 / (
                    jnp.sum(near, axis=1, keepdims=True) + jnp.sum(far, axis=1, keepdims=True)
                )
                rows = pl.ds(r * CHUNK, CHUNK)
                weights_v[b, h, rows, 0:BLOCK] = (near * share).astype(jnp.bfloat16)
                weights_v[b, h, rows, BLOCK:LIST] = (far * share).astype(jnp.bfloat16)

    def give(t, h):
        rows = pl.ds(pl.multiple_of(t * OWN_ROWS, OWN_ROWS), OWN_ROWS)
        part = out_v.at[rows, pl.ds(pl.multiple_of(h * HEAD_SIZE, HEAD_SIZE), HEAD_SIZE)]
        at = pl.multiple_of((head * GROUP + h) * HEAD_SIZE, HEAD_SIZE)
        spot = out_ref.at[:, pl.ds(at, HEAD_SIZE)]

        @pl.when(t != head)
        def _():
            remote(part, spot, out_send.at[t], out_recv, "head", t).start()

        @pl.when(t == head)
        def _():
            pltpu.make_async_copy(part, spot, out_local).start()

    def combine(b):
        drain(far_v.at[1, b, pl.ds(0, HALF - 1)], p2_recv.at[1, b])
        far_values = far_v[1, b].reshape(PICKS * BLOCK, HEAD_SIZE)
        rows = pl.ds(pl.multiple_of(b * BLOCK, BLOCK), BLOCK)
        near_values = vs_v[rows]

        @pl.loop(0, GROUP)
        def _(h):
            total = jnp.dot(
                weights_v[b, h, :, 0:BLOCK], near_values, preferred_element_type=jnp.float32
            ) + jnp.dot(
                weights_v[b, h, :, BLOCK:LIST], far_values, preferred_element_type=jnp.float32
            )
            out_v[rows, pl.ds(pl.multiple_of(h * HEAD_SIZE, HEAD_SIZE), HEAD_SIZE)] = (
                total.astype(jnp.bfloat16)
            )
            for i in range(GROUP):
                give(b * GROUP + i, h)

    for b in order:
        softmax(b)
    for b in order:
        combine(b)
    drain(out_ref.at[:, pl.ds(0, (N_HEAD - 1) * GROUP * HEAD_SIZE)], out_recv)
    for t in range(N_HEAD):
        part = out_v.at[pl.ds(t * OWN_ROWS, OWN_ROWS)]

        @pl.when(t != head)
        def _():
            drain(part, out_send.at[t])

        @pl.when(t == head)
        def _():
            drain(part, out_local)

    drain(all_v.at[pl.ds(0, NZ - 1)], ch_send.at[0])
    drain(all_v.at[pl.ds(0, (NX - 1) * NZ)], ch_send.at[1])
    for t in range(2):
        drain(column_v.at[t, pl.ds(HOT, HOT * (NX - 1))], p1_send.at[t])
        drain(tables[t].at[pl.ds(0, HOT * NX * (NZ - 1))], p1_send.at[t])
        for b in range(Q_BLOCKS):
            drain(send_v.at[t, b], p2_send.at[t])
            drain(far_v.at[t, b, pl.ds(0, HALF - 1)], p2_send.at[t])


def shards(queries, span_keys, span_values, cached_keys, cached_values, chosen):
    rows, width = queries.shape
    bf16 = jnp.bfloat16
    anywhere = pl.BlockSpec(memory_space=pl.ANY)
    dma = pltpu.SemaphoreType.DMA
    return pl.pallas_call(
        kernel,
        out_shape=pltpu.VMEM((rows // N_HEAD, width * N_HEAD), bf16),
        in_specs=[anywhere] * 5 + [pl.BlockSpec(memory_space=pltpu.SMEM)],
        out_specs=pl.BlockSpec(memory_space=pltpu.VMEM),
        scratch_shapes=[
            pltpu.VMEM((rows, width), bf16),
            pltpu.VMEM((rows, HEAD_SIZE), bf16),
            pltpu.VMEM((rows, HEAD_SIZE), bf16),
            pltpu.VMEM((DEV_BLOCKS, BLOCK, HEAD_SIZE), bf16),
            pltpu.VMEM((DEV_BLOCKS, BLOCK, HEAD_SIZE), bf16),
            pltpu.VMEM((2, HOT, BLOCK, HEAD_SIZE), bf16),
            pltpu.VMEM((2, HOT * NX, COLUMN, HEAD_SIZE), bf16),
            pltpu.VMEM((HOT * N_CTX, ROWS, HEAD_SIZE), bf16),
            pltpu.VMEM((HOT * N_CTX, ROWS, HEAD_SIZE), bf16),
            pltpu.VMEM((2, Q_BLOCKS, NX - 1, HALF, PICKS * ROWS, HEAD_SIZE), bf16),
            pltpu.VMEM((2, Q_BLOCKS, NX, HALF, PICKS * ROWS, HEAD_SIZE), bf16),
            pltpu.VMEM((2, Q_BLOCKS, HALF, NX, PICKS * ROWS, HEAD_SIZE), bf16),
            pltpu.VMEM((1, 1, 128), jnp.int32),
            pltpu.VMEM((N_CTX, 1, 128), jnp.int32),
            pltpu.VMEM((N_CTX, 128), jnp.int32),
            pltpu.SMEM((N_CTX, 128), jnp.int32),
            pltpu.VMEM((Q_BLOCKS, GROUP, BLOCK, LIST), bf16),
            pltpu.VMEM((rows, width), bf16),
            dma((5,)), dma, dma((2,)), dma((2,)), dma((2,)), dma((2,)), dma((2,)), dma((2, 2)),
            dma((2,)), dma((2, 2)), dma((N_HEAD,)), dma, dma,
        ],
        compiler_params=pltpu.CompilerParams(
            collective_id=0, has_side_effects=True, vmem_limit_bytes=56 << 20
        ),
        cost_estimate=pl.CostEstimate(
            flops=4 * rows * GROUP * LIST * HEAD_SIZE,
            bytes_accessed=8 << 20,
            transcendentals=rows * GROUP * LIST,
        ),
    )(
        queries, span_keys, span_values,
        cached_keys.reshape(DEV_BLOCKS, BLOCK, HEAD_SIZE),
        cached_values.reshape(DEV_BLOCKS, BLOCK, HEAD_SIZE),
        chosen,
    )


def solution(mesh):
    placed = (P("ctx", "head"),) * 5 + (P("ctx", "head", None),)
    return jax.shard_map(
        shards, mesh=mesh, in_specs=placed, out_specs=P(("ctx", "head"), None), check_vma=False
    )
```

```python
import functools
import math

import jax
import jax.numpy as jnp
from jax import lax
from jax.experimental import pallas as pl
from jax.experimental.pallas import tpu as pltpu
from jax.sharding import PartitionSpec as P

HEAD_SIZE = 128
BLOCK = 512
PICKS = 3
HOT = 2
NX, NZ = 4, 16
HALF = NZ // 2
FAR_X = (2, 1, 3)
REACH = HALF // 2
N_CTX = NX * NZ
N_HEAD = 8
SLICES = NX * HALF
ROWS = BLOCK // SLICES
COLUMN = BLOCK // NX
GROUP = 4
OWN_ROWS = 128
Q_BLOCKS = 2
DEV_BLOCKS = 8
LIST = BLOCK * (PICKS + 1)
CHUNK = 256
LOG2_SCALE = math.log2(math.e) / math.sqrt(HEAD_SIZE)
BIG = 1 << 20
MESH = pl.DeviceIdType.MESH


def dot_rows(left, right):
    return lax.dot_general(
        left, right, (((1,), (1,)), ((), ())), preferred_element_type=jnp.float32
    )


def remote(src, dst, send_sem, recv_sem, axis, peer):
    return pltpu.make_async_remote_copy(
        src_ref=src,
        dst_ref=dst,
        send_sem=send_sem,
        recv_sem=recv_sem,
        device_id={axis: peer},
        device_id_type=MESH,
    )


def drain(ref, sem):
    pltpu.make_async_copy(ref, ref, sem).wait()


def kernel(
    q_hbm, ks_hbm, vs_hbm, kc_hbm, vc_hbm, chosen_hbm, out_ref,
    q_v, ks_v, vs_v, cache_k, cache_w, hot_v, column_v, table_k, table_w, send_v, relay_v, far_v,
    chosen_s, row_v, all_v, index_v, index_s, weights_v, out_v,
    load_sem, index_sem, ch_send, ch_recv, p1_send, p1_recv, p2_send, p2_recv,
    x1_recv, x2_recv, out_send, out_recv, out_local,
):
    me = lax.axis_index("ctx")
    head = lax.axis_index("head")
    mx, mz = me // NZ, me % NZ
    mine_at = mz % HALF
    caches, tables = (cache_k, cache_w), (table_k, table_w)

    def along_x(d):
        return (mx + d) % NX * NZ + mz

    def along_z(d):
        return mx * NZ + (mz + d) % NZ

    own = pltpu.make_async_copy(chosen_hbm, chosen_s, index_sem)
    own.start()

    def far_first(i):
        return HALF + (i + 1) // 2 * (1 - i % 2 * 2)

    barrier = pltpu.get_barrier_semaphore()

    def greet(axis, peer):
        pl.semaphore_signal(barrier, inc=1, device_id={axis: peer}, device_id_type=MESH)

    @pl.loop(0, NZ - 1)
    def _(i):
        greet("ctx", along_z(far_first(i)))

    for d in FAR_X:
        greet("ctx", along_x(d))

    @pl.loop(1, N_HEAD)
    def _(i):
        greet("head", (head + i) % N_HEAD)

    own.wait()
    lane = lax.broadcasted_iota(jnp.int32, (1, 128), 1)
    mine = jnp.full((1, 128), -1, jnp.int32)
    for b in range(Q_BLOCKS):
        for j in range(PICKS):
            mine = jnp.where(lane == b * PICKS + j, chosen_s[b, 0, j], mine)
    row_v[0] = mine
    all_v[me] = mine
    pl.semaphore_wait(barrier, NZ - 1 + NX - 1 + N_HEAD - 1)

    @pl.loop(0, NZ - 1)
    def _(i):
        remote(
            row_v.at[0], all_v.at[me], ch_send.at[0], ch_recv.at[0], "ctx",
            along_z(far_first(i)),
        ).start()

    loads = [
        pltpu.make_async_copy(kc_hbm, cache_k, load_sem.at[0]),
        pltpu.make_async_copy(vc_hbm, cache_w, load_sem.at[1]),
        pltpu.make_async_copy(q_hbm, q_v, load_sem.at[2]),
        pltpu.make_async_copy(ks_hbm, ks_v, load_sem.at[3]),
        pltpu.make_async_copy(vs_hbm, vs_v, load_sem.at[4]),
    ]
    for load in loads[:2]:
        load.start()

    drain(all_v.at[pl.ds(0, NZ - 1)], ch_recv.at[0])
    column = all_v.at[pl.ds(mx * NZ, NZ)]

    for d in FAR_X:
        remote(column, column, ch_send.at[1], ch_recv.at[1], "ctx", along_x(d)).start()

    drain(all_v.at[pl.ds(0, (NX - 1) * NZ)], ch_recv.at[1])
    picked = all_v[...].reshape(N_CTX, 128)
    owner = jnp.where(picked < 0, -1, picked // DEV_BLOCKS)
    here = owner == me
    low = jnp.min(jnp.where(here, picked, BIG))
    high = jnp.max(jnp.where(here, picked, -1))
    first = me * DEV_BLOCKS
    low = jnp.clip(low - first, 0, DEV_BLOCKS - 1)
    high = jnp.clip(high - first, 0, DEV_BLOCKS - 1)

    def spread_x(t):
        loads[t].wait()
        hot_v[t, 0] = caches[t][low]
        hot_v[t, 1] = caches[t][high]
        for d in range(1, NX):
            at = pl.multiple_of((mx + d) % NX * COLUMN, COLUMN)
            remote(
                hot_v.at[t, :, pl.ds(at, COLUMN)],
                column_v.at[t, pl.ds((NX - d) * HOT, HOT)],
                p1_send.at[t], x1_recv.at[t], "ctx", along_x(d),
            ).start()
        at = pl.multiple_of(mx * COLUMN, COLUMN)
        column_v[t, 0:HOT] = hot_v[t, :, pl.ds(at, COLUMN)]

    def spread_z(t, start, count):
        @pl.loop(0, NZ - 1)
        def _(i):
            i = far_first(i)
            at = pl.multiple_of((mz + i) % HALF * ROWS, ROWS)
            remote(
                column_v.at[t, pl.ds(start, count), pl.ds(at, ROWS)],
                tables[t].at[pl.ds(mz * HOT * NX + start, count)],
                p1_send.at[t], p1_recv.at[t], "ctx", along_z(i),
            ).start()

        at = pl.multiple_of(mine_at * ROWS, ROWS)
        tables[t][pl.ds(mz * HOT * NX + start, count)] = column_v[
            t, pl.ds(start, count), pl.ds(at, ROWS)
        ]

    spread_x(0)
    spread_z(0, 0, HOT)
    spread_x(1)
    drain(column_v.at[0, pl.ds(HOT, HOT * (NX - 1))], x1_recv.at[0])
    spread_z(0, HOT, HOT * (NX - 1))
    drain(column_v.at[1, pl.ds(HOT, HOT * (NX - 1))], x1_recv.at[1])
    spread_z(1, 0, HOT * NX)

    for load in loads[2:]:
        load.start()

    lane_c = lax.broadcasted_iota(jnp.int32, (N_CTX, 128), 1)
    lows = jnp.full((1, 128), BIG, jnp.int32)
    for e in range(Q_BLOCKS * PICKS):
        hit = owner[:, e : e + 1] == lane_c
        lows = jnp.minimum(
            lows, jnp.min(jnp.where(hit, picked[:, e : e + 1], BIG), axis=0, keepdims=True)
        )
    index = jnp.zeros((N_CTX, 128), jnp.int32)
    for e in range(Q_BLOCKS * PICKS):
        at = owner[:, e : e + 1]
        hit = at == lane_c
        least = jnp.min(jnp.where(hit, lows, BIG), axis=1, keepdims=True)
        later = (picked[:, e : e + 1] != least).astype(jnp.int32)
        spot = (at % NZ * NX + (at // NZ + NX - mx) % NX) * HOT + later
        index = jnp.where(lane_c == e, spot, index)
    index_v[...] = index
    to_scalar = pltpu.make_async_copy(index_v, index_s, index_sem)
    to_scalar.start()
    to_scalar.wait()

    def fill(t, b, peer, ref):
        for j in range(PICKS):
            ref[pl.ds(j * ROWS, ROWS)] = tables[t][index_s[peer, b * PICKS + j]]

    def z_shift(b, k):
        return k + NZ - (REACH - 1 + b)

    def deliver_x(t, b):
        @pl.loop(0, HALF)
        def _(k):
            fill(t, b, along_z(z_shift(b, k)), relay_v.at[t, b, 0, k])

        for d in range(1, NX):
            @pl.loop(0, HALF)
            def _(k):
                peer = (mx + d) % NX * NZ + (mz + z_shift(b, k)) % NZ
                fill(t, b, peer, send_v.at[t, b, d - 1, k])

            remote(
                send_v.at[t, b, d - 1], relay_v.at[t, b, NX - d],
                p2_send.at[t], x2_recv.at[t, b], "ctx", along_x(d),
            ).start()

    def deliver_z(t, b):
        drain(relay_v.at[t, b, pl.ds(1, NX - 1)], x2_recv.at[t, b])
        stay = REACH - 1 + b

        @pl.loop(0, HALF - 1)
        def _(i):
            k = (stay + 3 + i * 3) % HALF
            remote(
                relay_v.at[t, b, :, k], far_v.at[t, b, mine_at],
                p2_send.at[t], p2_recv.at[t, b], "ctx", along_z(z_shift(b, k)),
            ).start()

        far_v[t, b, mine_at] = relay_v[t, b, :, stay]

    lead = 1 - head // (N_HEAD // 2)
    order = (lead, 1 - lead)
    for t in range(2):
        drain(tables[t].at[pl.ds(0, HOT * NX * (NZ - 1))], p1_recv.at[t])

        @pl.loop(0, Q_BLOCKS)
        def _(i):
            deliver_x(t, (lead + i) % Q_BLOCKS)

        @pl.loop(0, Q_BLOCKS)
        def _(i):
            deliver_z(t, (lead + i) % Q_BLOCKS)

    for load in loads[2:]:
        load.wait()

    def softmax(b):
        drain(far_v.at[0, b, pl.ds(0, HALF - 1)], p2_recv.at[0, b])
        far_keys = far_v[0, b].reshape(PICKS * BLOCK, HEAD_SIZE)
        near_keys = ks_v[pl.ds(pl.multiple_of(b * BLOCK, BLOCK), BLOCK)]

        @pl.loop(0, GROUP)
        def _(h):
            @pl.loop(0, BLOCK // CHUNK)
            def _(r):
                query = q_v[
                    pl.ds(pl.multiple_of(b * BLOCK + r * CHUNK, CHUNK), CHUNK),
                    pl.ds(pl.multiple_of(h * HEAD_SIZE, HEAD_SIZE), HEAD_SIZE),
                ]
                near = dot_rows(query, near_keys)
                below = (
                    r * CHUNK + lax.broadcasted_iota(jnp.int32, (CHUNK, BLOCK), 0)
                    >= lax.broadcasted_iota(jnp.int32, (CHUNK, BLOCK), 1)
                )
                near = jnp.where(below, near, -jnp.inf)
                far = dot_rows(query, far_keys)
                top = jnp.maximum(
                    jnp.max(near, axis=1, keepdims=True), jnp.max(far, axis=1, keepdims=True)
                )
                near = jnp.exp2((near - top) * LOG2_SCALE)
                far = jnp.exp2((far - top) * LOG2_SCALE)
                share = 1.0 / (
                    jnp.sum(near, axis=1, keepdims=True) + jnp.sum(far, axis=1, keepdims=True)
                )
                rows = pl.ds(pl.multiple_of(r * CHUNK, CHUNK), CHUNK)
                weights_v[b, h, rows, 0:BLOCK] = (near * share).astype(jnp.bfloat16)
                weights_v[b, h, rows, BLOCK:LIST] = (far * share).astype(jnp.bfloat16)

    def give(t, h):
        rows = pl.ds(pl.multiple_of(t * OWN_ROWS, OWN_ROWS), OWN_ROWS)
        part = out_v.at[rows, pl.ds(pl.multiple_of(h * HEAD_SIZE, HEAD_SIZE), HEAD_SIZE)]
        at = pl.multiple_of((head * GROUP + h) * HEAD_SIZE, HEAD_SIZE)
        spot = out_ref.at[:, pl.ds(at, HEAD_SIZE)]

        @pl.when(t != head)
        def _():
            remote(part, spot, out_send.at[t], out_recv, "head", t).start()

        @pl.when(t == head)
        def _():
            pltpu.make_async_copy(part, spot, out_local).start()

    def combine(b):
        drain(far_v.at[1, b, pl.ds(0, HALF - 1)], p2_recv.at[1, b])
        far_values = far_v[1, b].reshape(PICKS * BLOCK, HEAD_SIZE)
        rows = pl.ds(pl.multiple_of(b * BLOCK, BLOCK), BLOCK)
        near_values = vs_v[rows]

        @pl.loop(0, GROUP)
        def _(h):
            total = jnp.dot(
                weights_v[b, h, :, 0:BLOCK], near_values, preferred_element_type=jnp.float32
            ) + jnp.dot(
                weights_v[b, h, :, BLOCK:LIST], far_values, preferred_element_type=jnp.float32
            )
            out_v[rows, pl.ds(pl.multiple_of(h * HEAD_SIZE, HEAD_SIZE), HEAD_SIZE)] = (
                total.astype(jnp.bfloat16)
            )
            for i in range(GROUP):
                give(b * GROUP + i, h)

    @pl.loop(0, Q_BLOCKS)
    def _(i):
        softmax((lead + i) % Q_BLOCKS)

    @pl.loop(0, Q_BLOCKS)
    def _(i):
        combine((lead + i) % Q_BLOCKS)

    drain(out_ref.at[:, pl.ds(0, (N_HEAD - 1) * GROUP * HEAD_SIZE)], out_recv)
    for t in range(N_HEAD):
        part = out_v.at[pl.ds(t * OWN_ROWS, OWN_ROWS)]

        @pl.when(t != head)
        def _():
            drain(part, out_send.at[t])

        @pl.when(t == head)
        def _():
            drain(part, out_local)

    drain(all_v.at[pl.ds(0, NZ - 1)], ch_send.at[0])
    drain(all_v.at[pl.ds(0, (NX - 1) * NZ)], ch_send.at[1])
    for t in range(2):
        drain(column_v.at[t, pl.ds(HOT, HOT * (NX - 1))], p1_send.at[t])
        drain(tables[t].at[pl.ds(0, HOT * NX * (NZ - 1))], p1_send.at[t])
        for b in range(Q_BLOCKS):
            drain(send_v.at[t, b], p2_send.at[t])
            drain(far_v.at[t, b, pl.ds(0, HALF - 1)], p2_send.at[t])


def shards(queries, span_keys, span_values, cached_keys, cached_values, chosen):
    rows, width = queries.shape
    bf16 = jnp.bfloat16
    anywhere = pl.BlockSpec(memory_space=pl.ANY)
    dma = pltpu.SemaphoreType.DMA
    return pl.pallas_call(
        kernel,
        out_shape=pltpu.VMEM((rows // N_HEAD, width * N_HEAD), bf16),
        in_specs=[anywhere] * 6,
        out_specs=pl.BlockSpec(memory_space=pltpu.VMEM),
        scratch_shapes=[
            pltpu.VMEM((rows, width), bf16),
            pltpu.VMEM((rows, HEAD_SIZE), bf16),
            pltpu.VMEM((rows, HEAD_SIZE), bf16),
            pltpu.VMEM((DEV_BLOCKS, BLOCK, HEAD_SIZE), bf16),
            pltpu.VMEM((DEV_BLOCKS, BLOCK, HEAD_SIZE), bf16),
            pltpu.VMEM((2, HOT, BLOCK, HEAD_SIZE), bf16),
            pltpu.VMEM((2, HOT * NX, COLUMN, HEAD_SIZE), bf16),
            pltpu.VMEM((HOT * N_CTX, ROWS, HEAD_SIZE), bf16),
            pltpu.VMEM((HOT * N_CTX, ROWS, HEAD_SIZE), bf16),
            pltpu.VMEM((2, Q_BLOCKS, NX - 1, HALF, PICKS * ROWS, HEAD_SIZE), bf16),
            pltpu.VMEM((2, Q_BLOCKS, NX, HALF, PICKS * ROWS, HEAD_SIZE), bf16),
            pltpu.VMEM((2, Q_BLOCKS, HALF, NX, PICKS * ROWS, HEAD_SIZE), bf16),
            pltpu.SMEM(chosen.shape, jnp.int32),
            pltpu.VMEM((1, 1, 128), jnp.int32),
            pltpu.VMEM((N_CTX, 1, 128), jnp.int32),
            pltpu.VMEM((N_CTX, 128), jnp.int32),
            pltpu.SMEM((N_CTX, 128), jnp.int32),
            pltpu.VMEM((Q_BLOCKS, GROUP, BLOCK, LIST), bf16),
            pltpu.VMEM((rows, width), bf16),
            dma((5,)), dma, dma((2,)), dma((2,)), dma((2,)), dma((2,)), dma((2,)), dma((2, 2)),
            dma((2,)), dma((2, 2)), dma((N_HEAD,)), dma, dma,
        ],
        compiler_params=pltpu.CompilerParams(
            collective_id=0, has_side_effects=True, vmem_limit_bytes=56 << 20
        ),
        cost_estimate=pl.CostEstimate(
            flops=4 * rows * GROUP * LIST * HEAD_SIZE,
            bytes_accessed=8 << 20,
            transcendentals=rows * GROUP * LIST,
        ),
    )(
        queries, span_keys, span_values,
        cached_keys.reshape(DEV_BLOCKS, BLOCK, HEAD_SIZE),
        cached_values.reshape(DEV_BLOCKS, BLOCK, HEAD_SIZE),
        chosen,
    )


def solution(mesh):
    placed = (P("ctx", "head"),) * 5 + (P("ctx", "head", None),)
    return jax.shard_map(
        shards, mesh=mesh, in_specs=placed, out_specs=P(("ctx", "head"), None), check_vma=False
    )
```
